32 devices in a mesh: sub: 8 (over z, x), agg: 4 (over y, core).
Axes of the slice: x: 2, y: 2, z: 4, core: 2. Of those that a mesh axis runs over, the one named last changes fastest.
Arguments:
- dual_load: float32 [4, 8, 64, 1536], P('agg', 'sub'), may hold values from -58 to 58
- interface_inverse: bfloat16 [4, 8, 1536, 1536], P('agg', 'sub'), may hold values from -1 to 2.5, as said below
- dirichlet: bfloat16 [4, 8, 1536, 1536], P('agg', 'sub'), may hold values from -1 to 2.5, as said below
- coupling: bfloat16 [4, 8, 128, 1536], P('agg', 'sub'), may hold values from -0.15625 to 0.15625
- neighbours: int32 [4, 8, 8], P('agg', 'sub'), may hold values from -1 to 7, as said below
- face_counts: int32 [4, 8, 8], P('agg', 'sub'), may hold values from 0 to 192, as said below
- owners: int32 [4, 8, 128, 1], P('agg', 'sub'), may hold values from 0 to 3; in each aligned block of 128 rows (0 to 127, 128 to 255, ..., all dimensions but the last counted through in order) at most 48 rows name the same one
- primal_rows: int32 [4, 8, 128], P('agg', 'sub'), may hold values from 0 to 1023
- coarse_inverse: float32 [4, 1024, 1024], P('agg', 'sub'), may hold values from -1 to 1.5, as said below
Outputs:
- solution: float32 [4, 8, 64, 1536], P('agg', 'sub')
- residual: float32 [4, 8, 64, 1536], P('agg', 'sub')
The draws below stay inside these ranges and needn't reach their ends.
Inputs may be any that keep to these rules, and one draw needn't show every extreme that they name: `neighbours`: each subdomain lists peers of its own aggregate by their index along sub, -1 in empty slots; no peer twice; if j lists i then i lists j; every listed peer lies within a cyclic distance of 3 along sub. `face_counts`: 0 exactly in empty slots, 48 or more elsewhere; both sides of a face give the same count and hold its rows in the same order. `owners`: among the 128 primal rows of one subdomain no aggregate is named more than 48 times. `interface_inverse`: each subdomain's matrix is symmetric positive definite. `dirichlet`: each subdomain's matrix is symmetric positive definite. `coarse_inverse`: each aggregate's matrix is symmetric positive definite.
All inputs are finite; a program needn't handle non-finite values.
Results may differ from the reference program's by a relative error of at most 0.011.
Values sent between devices are 32-bit elements; how exact they have to be, the bound alone decides.
A program may use at most 128 MiB of HBM per device.

```python
import math
import jax
import jax.numpy as jnp
import numpy as np
from jax import lax

NB = 8
FMAX = 192
NI = 1536
NRHS = 64
NP = 128
NC = 1024
CAP = 48
ITERS = 2
REACH = 3
N_SUB = 8
N_AGG = 4


def spd_block(key, order, lowest, highest, spread):
    first, second = jax.random.split(key)
    noise = jnp.clip(jax.random.normal(first, (order, order), jnp.float32), -4.0, 4.0)
    diagonal = jax.random.uniform(second, (order,), jnp.float32, lowest, highest)
    symmetric = (noise + noise.T) * (spread / math.sqrt(2.0 * order))
    return symmetric + jnp.diag(diagonal)


def draw_interface_inverse(key, part):

    def single(index):
        return spd_block(jax.random.fold_in(jax.random.fold_in(key, 11), index), NI, 1.0, 2.0, 0.4).astype(jnp.bfloat16)
    blocks = lax.map(single, jnp.arange(N_AGG * N_SUB, dtype=jnp.int32))
    return blocks.reshape(N_AGG, N_SUB, NI, NI)


def draw_dirichlet(key, part):

    def single(index):
        return spd_block(jax.random.fold_in(jax.random.fold_in(key, 23), index), NI, 1.0, 2.0, 0.35).astype(jnp.bfloat16)
    blocks = lax.map(single, jnp.arange(N_AGG * N_SUB, dtype=jnp.int32))
    return blocks.reshape(N_AGG, N_SUB, NI, NI)


def draw_coarse_inverse(key, part):

    def single(index):
        return spd_block(jax.random.fold_in(jax.random.fold_in(key, 37), index), NC, 0.5, 1.0, 0.2)
    return lax.map(single, jnp.arange(N_AGG, dtype=jnp.int32))


def draw_dual_load(key, part):
    first, second, third = jax.random.split(jax.random.fold_in(key, 5), 3)
    shape = (N_AGG, N_SUB, NRHS, NI)
    base = jnp.clip(jax.random.normal(first, shape, jnp.float32), -3.0, 3.0)
    row_scale = jnp.exp(jax.random.uniform(second, (1, 1, 1, NI), jnp.float32, -1.15, 1.15))
    case_scale = jnp.exp(jax.random.uniform(third, (1, 1, NRHS, 1), jnp.float32, -0.7, 0.7))
    place = jnp.arange(N_AGG * N_SUB, dtype=jnp.float32).reshape(N_AGG, N_SUB, 1, 1) / max(N_AGG * N_SUB - 1, 1)
    rising = jnp.exp(math.log(3.0) * place)
    return base * row_scale * case_scale * rising


def face_graph(key):
    first, second = jax.random.split(jax.random.fold_in(key, 77))
    keep = jax.random.randint(first, (N_AGG, REACH, N_SUB), 0, 5) < 4
    sizes = jax.random.randint(second, (N_AGG, REACH, N_SUB), FMAX // 4, FMAX + 1)
    keep = keep.at[:, 0, 0].set(True)
    keep = keep.at[:, REACH - 1, 1].set(False)
    sizes = sizes.at[:, 0, 0].set(FMAX)
    peers = jnp.arange(N_SUB, dtype=jnp.int32)[None, :]
    lists = []
    counts = []
    for offset in range(REACH):
        distance = offset + 1
        lists.append(jnp.where(keep[:, offset], (peers + distance) % N_SUB, -1))
        counts.append(jnp.where(keep[:, offset], sizes[:, offset], 0))
        back_keep = jnp.roll(keep[:, offset], distance, axis=1)
        back_size = jnp.roll(sizes[:, offset], distance, axis=1)
        lists.append(jnp.where(back_keep, (peers + N_SUB - distance) % N_SUB, -1))
        counts.append(jnp.where(back_keep, back_size, 0))
    for filler in range(NB - 2 * REACH):
        lists.append(jnp.full((N_AGG, N_SUB), -1, jnp.int32))
        counts.append(jnp.zeros((N_AGG, N_SUB), jnp.int32))
    return (jnp.stack(lists, axis=-1).astype(jnp.int32), jnp.stack(counts, axis=-1).astype(jnp.int32))


def draw_neighbours(key, part):
    return face_graph(key)[0]


def draw_face_counts(key, part):
    return face_graph(key)[1]


def set_ends(drawn, key, low, top_value):
    extent = drawn.shape
    index_at = [jax.random.randint(jax.random.fold_in(key, axis), (), 0, extent[axis]) for axis in range(len(extent))]
    drawn = drawn.at[tuple(index_at)].set(low)
    longest = extent.index(max(extent))
    index_at[longest] = (index_at[longest] + 1) % extent[longest]
    return drawn.at[tuple(index_at)].set(top_value)


def levels(rng, dims, cuts, least, top_value):
    def one(position, parts):
        draws = jax.random.uniform(jax.random.fold_in(jax.random.fold_in(rng, 6), position), (parts,), jnp.float32, least / len(cuts), top_value / len(cuts))
        return jnp.repeat(jnp.exp(draws), dims[position] // parts).reshape((-1,) + (1,) * (len(dims) - position - 1))

    factor_of = one(*cuts[0])
    for cut in cuts[1:]:
        factor_of = factor_of * one(*cut)
    return factor_of


def deal_out(rng, own, number, rows, count, top, limit, slope):
    sequence = jax.random.permutation(rng, count)
    heavy_load, ordinary = load_shares(count, rows * top, limit, slope, True), load_shares(count, rows * top, limit, slope, False)
    places = jnp.arange(count)

    def named(lengths, turn):
        used = int((lengths > 0).sum())
        fixed = max(1, used // 4)
        passed = fixed + (places - fixed + turn * (used - fixed)) % max(1, count - fixed)
        return jnp.zeros((count,), jnp.int32).at[sequence[jnp.where(places < fixed, places, passed)]].set(jnp.asarray(lengths, jnp.int32))

    lengths = jnp.where(number % 4 == 0, named(heavy_load, number // 4), named(ordinary, number - number // 4 - 1))
    mixed = jax.random.permutation(jax.random.fold_in(own, 3), count)
    giver, sink = mixed[0:count // 2 * 2:2], mixed[1:count // 2 * 2:2]
    room = jnp.minimum(lengths[giver] - 1, limit - lengths[sink]) // 2
    room = jnp.where((giver == sequence[0]) | (sink == sequence[0]) | (lengths[sink] == 0), 0, jnp.maximum(room, 0))
    passed = jax.random.randint(jax.random.fold_in(own, 4), (count // 2,), 0, 1 << 20) % (room + 1)
    lengths = lengths.at[giver].add(-passed).at[sink].add(passed)
    items = jnp.searchsorted(jnp.cumsum(lengths), jnp.arange(rows * top), side="right").astype(jnp.int32)
    table = items.reshape(top, rows).T
    table = table[jax.random.permutation(jax.random.fold_in(own, 1), rows)]
    turn = jax.random.randint(jax.random.fold_in(own, 2), (rows, 1), 0, top)
    return jnp.take_along_axis(table, (jnp.arange(top)[None, :] + turn) % top, axis=1)


def load_shares(amount, total, limit, lean, full):
    portions = [(1 << 20) // math.isqrt(standing ** lean) + 1 for standing in range(1, amount + 1)]
    largest = limit if full else min(limit, max(-(-total // amount), total * portions[0] // sum(portions)))
    least = 1 if total - largest >= amount - 1 else 0
    given, surplus = [largest] + [least] * (amount - 1), total - largest - least * (amount - 1)
    while surplus > 0:
        free = [i for i in range(1, amount) if given[i] < largest] or [i for i in range(1, amount) if given[i] < limit]
        whole, budget = sum([portions[i] for i in free]), surplus
        for i in free:
            addition = min(limit - given[i], max(1, budget * portions[i] // whole), surplus)
            given[i] = given[i] + addition
            surplus = surplus - addition
    return np.array(given)


def bell_draw(stream_key, shape, scale, most, cuts=(), kind=jnp.bfloat16):
    result = jax.random.normal(stream_key, shape, jnp.float32) * scale
    if len(cuts) > 0:
        result = levels(stream_key, shape, cuts, -0.22, 0.18) * result
    return jnp.clip(result, min=-most, max=most).astype(kind)


def setup_inputs(seed: int = 0) -> dict:
    key_list = jax.random.split(jax.random.key(seed), 10)
    dual_load = draw_dual_load(jax.random.fold_in(key_list[9], 71), 0)
    interface_inverse = draw_interface_inverse(jax.random.fold_in(key_list[9], 71), 0)
    dirichlet = draw_dirichlet(jax.random.fold_in(key_list[9], 71), 0)
    coupling = bell_draw(key_list[3], (N_AGG, N_SUB, NP, NI), NI ** -0.5, 0.15625, ((0, 4), (1, 8)))
    neighbours = draw_neighbours(jax.random.fold_in(key_list[9], 71), 0)
    face_counts = draw_face_counts(jax.random.fold_in(key_list[9], 71), 0)
    owners_keys = jax.random.split(jax.random.fold_in(key_list[6], 1), N_AGG * N_SUB * NP // NP)
    owners_turns = jax.random.permutation(jax.random.fold_in(key_list[6], 3), N_AGG * N_SUB * NP // NP)
    owners = jax.vmap(lambda own, number: deal_out(jax.random.fold_in(key_list[6], 2), own, number, NP, N_AGG, 1, CAP, 2))(owners_keys, owners_turns).reshape((N_AGG, N_SUB, NP, 1))
    primal_rows = set_ends(jax.random.randint(key_list[7], (N_AGG, N_SUB, NP), 0, NC), jax.random.fold_in(key_list[7], 1), 0, NC - 1).astype(jnp.int32)
    coarse_inverse = draw_coarse_inverse(jax.random.fold_in(key_list[9], 71), 0)
    return {"dual_load": dual_load, "interface_inverse": interface_inverse, "dirichlet": dirichlet, "coupling": coupling, "neighbours": neighbours, "face_counts": face_counts, "owners": owners, "primal_rows": primal_rows, "coarse_inverse": coarse_inverse}


FULL_PRECISION = lax.Precision.HIGHEST
CONTRACT_LAST = (((1,), (1,)), ((), ()))


def row_mask(face_counts):
    depth = jnp.arange(FMAX, dtype=jnp.int32)
    inside = depth[None, None, None, :] < face_counts[:, :, :, None]
    return inside.reshape(N_AGG, N_SUB, 1, NI).astype(jnp.float32)


def link_table(neighbours):
    peers = jnp.arange(N_SUB, dtype=jnp.int32)
    goes = neighbours[:, :, :, None] == peers[None, None, None, :]
    back = jnp.transpose(goes, (0, 3, 1, 2))
    table = goes[:, :, :, :, None] & back[:, :, None, :, :]
    return table.astype(jnp.float32)


def assemble(local, links, mask):
    faces = local.reshape(N_AGG, N_SUB, NRHS, NB, FMAX)

    def per_aggregate(operands):
        return jnp.einsum("ikjl,jrlf->irkf", operands[1], operands[0], precision=FULL_PRECISION)

    incoming = lax.map(per_aggregate, (faces, links))
    return mask * (local + incoming.reshape(local.shape))


def batched_dot(left, right):
    return lax.map(lambda operands: jnp.dot(operands[0], operands[1], preferred_element_type=jnp.float32), (left, right))


def coarse_values(terms, owners, primal_rows, coarse_inverse):
    target = (owners.reshape(-1) * NC + primal_rows.reshape(-1)).astype(jnp.int32)
    columns = jnp.transpose(terms, (0, 2, 1)).reshape(-1, NRHS)
    summed = jax.ops.segment_sum(columns, target, num_segments=N_AGG * NC).reshape(N_AGG, NC, NRHS)
    solved = jnp.einsum("acd,adr->acr", coarse_inverse, summed, precision=FULL_PRECISION)
    picked = solved.reshape(N_AGG * NC, NRHS)[target]
    return jnp.transpose(picked.reshape(-1, NP, NRHS), (0, 2, 1))


def reference(dual_load, interface_inverse, dirichlet, coupling, neighbours, face_counts, owners, primal_rows, coarse_inverse):
    mask = row_mask(face_counts)
    links = link_table(neighbours)
    inverse_flat = interface_inverse.reshape(-1, NI, NI)
    dirichlet_flat = dirichlet.reshape(-1, NI, NI)
    coupling_flat = coupling.reshape(-1, NP, NI)

    def operator(field):
        packed = field.reshape(-1, NRHS, NI).astype(jnp.bfloat16)
        own = batched_dot(packed, inverse_flat)
        terms = lax.map(lambda operands: lax.dot_general(operands[0], operands[1], CONTRACT_LAST, preferred_element_type=jnp.float32), (packed, coupling_flat))
        local_back = coarse_values(terms, owners, primal_rows, coarse_inverse).astype(jnp.bfloat16)
        correction = batched_dot(local_back, coupling_flat)
        local = mask * (own + correction).reshape(N_AGG, N_SUB, NRHS, NI)
        return assemble(local, links, mask)

    def precondition(field):
        packed = field.reshape(-1, NRHS, NI).astype(jnp.bfloat16)
        local = mask * batched_dot(packed, dirichlet_flat).reshape(N_AGG, N_SUB, NRHS, NI)
        return assemble(local, links, mask)

    def inner(first, second):
        return jnp.sum(first * second, axis=(0, 1, 3))

    rhs = assemble(mask * dual_load, links, mask)
    solution = jnp.zeros_like(rhs)
    residual = rhs
    precond = precondition(residual)
    direction = precond
    residual_dot = inner(residual, precond)
    for iteration in range(ITERS):
        image = operator(direction)
        alpha = (residual_dot / inner(direction, image))[None, None, :, None]
        solution = solution + alpha * direction
        residual = residual - alpha * image
        if iteration + 1 < ITERS:
            precond = precondition(residual)
            next_dot = inner(residual, precond)
            direction = precond + (next_dot / residual_dot)[None, None, :, None] * direction
            residual_dot = next_dot
    return solution, residual
```

```python
import functools

import jax
import jax.numpy as jnp
from jax import lax
from jax.experimental import pallas as pl
from jax.experimental.pallas import tpu as pltpu
from jax.sharding import PartitionSpec as P

CAP = 48
ITERS = 2
MESH = pl.DeviceIdType.MESH
F32 = jnp.float32
BF16 = jnp.bfloat16
NT = (((1,), (1,)), ((), ()))


def dot(left, right):
    return jnp.dot(left, right, preferred_element_type=F32)


def pack(face):
    cases, depth = face.shape
    whole = depth // 128 * 128
    half = cases // 2
    parts = [face[:, at : at + 128] for at in range(0, whole, 128)]
    if depth > whole:
        parts.append(jnp.concatenate([face[:half, whole:], face[half:, whole:]], axis=1))
    return jnp.concatenate(parts, axis=0)


def unpack(rows, cases, depth):
    whole = depth // 128 * 128
    parts = [rows[at * cases : (at + 1) * cases] for at in range(whole // 128)]
    if depth > whole:
        last = rows[whole // 128 * cases :]
        wide = depth - whole
        parts.append(jnp.concatenate([last[:, :wide], last[:, wide:]], axis=0))
    return jnp.concatenate(parts, axis=1)


def kernel(
    ns,
    na,
    reach,
    dual_ref,
    inverse_hbm,
    dirichlet_hbm,
    coupling_ref,
    peers_ref,
    counts_ref,
    owners_ref,
    rows_ref,
    coarse_ref,
    solution_ref,
    residual_ref,
    inverse_ref,
    dirichlet_ref,
    local_ref,
    field_ref,
    direction_ref,
    packed_ref,
    face_out,
    face_in,
    face_ss,
    face_rs,
    load_sem,
    cp_ref,
    mask_ref,
    ida_out,
    ida_in,
    ida_ss,
    ida_rs,
    idb_out,
    idb_in,
    idb_ss,
    idb_rs,
    hi_ref,
    lo_ref,
    pick_ref,
    a_out,
    a_in,
    a_ss,
    a_rs,
    b_out,
    b_in,
    b_ss,
    b_rs,
    s_out,
    s_in,
    s_ss,
    s_rs,
    r_out,
    r_in,
    r_ss,
    r_rs,
    du_out,
    du_in,
    du_ss,
    du_rs,
    dv_out,
    dv_in,
    dv_ss,
    dv_rs,
):
    cases, order = dual_ref.shape
    slots = peers_ref.shape[0]
    depth = order // slots
    primal = coupling_ref.shape[0]
    crow, nc = coarse_ref.shape
    half = CAP // 2
    used = na * half
    wide = ida_in.shape[2]
    sub = lax.axis_index("sub")
    agg = lax.axis_index("agg")

    def start(axis, src_of, dst, ss, rs):
        me, n = (sub, ns) if axis == "sub" else (agg, na)

        @pl.loop(1, n)
        def _(t):
            peer = lax.rem(me + t, n)
            pltpu.make_async_remote_copy(
                src_ref=src_of(peer),
                dst_ref=dst.at[me],
                send_sem=ss.at[t - 1],
                recv_sem=rs.at[t - 1],
                device_id={axis: peer},
                device_id_type=MESH,
            ).start()

    def receive(axis, src_of, dst, ss, rs):
        me, n = (sub, ns) if axis == "sub" else (agg, na)

        @pl.loop(1, n)
        def _(t):
            peer = lax.rem(me - t + n, n)
            copy = pltpu.make_async_remote_copy(
                src_ref=src_of(peer),
                dst_ref=dst.at[peer],
                send_sem=ss.at[t - 1],
                recv_sem=rs.at[t - 1],
                device_id={axis: peer},
                device_id_type=MESH,
            )
            copy.wait_recv()
            copy.wait_send()

    barrier = pltpu.get_barrier_semaphore()
    for axis, me, n in (("sub", sub, ns), ("agg", agg, na)):

        @pl.loop(1, n)
        def _(t, axis=axis, me=me, n=n):
            pl.semaphore_signal(
                barrier, inc=1, device_id={axis: lax.rem(me + t, n)}, device_id_type=MESH
            )

    load_d = pltpu.make_async_copy(dirichlet_hbm, dirichlet_ref, load_sem.at[0])
    load_k = pltpu.make_async_copy(inverse_hbm, inverse_ref, load_sem.at[1])
    load_d.start()
    load_k.start()

    lane = lax.broadcasted_iota(jnp.int32, (1, order), 1)
    mask = jnp.zeros((1, order), F32)
    for k in range(slots):
        inside = (lane >= k * depth) & (lane < k * depth + counts_ref[k])
        mask = mask + jnp.where(inside, 1.0, 0.0)
    mask_ref[...] = jnp.broadcast_to(mask, mask_ref.shape)

    hops = []
    for distance in range(1, reach + 1):
        ahead = lax.rem(sub + distance, ns)
        behind = lax.rem(sub + ns - distance, ns)
        hops.append((ahead, behind))
        hops.append((behind, ahead))
    weights = [
        [jnp.where(peers_ref[k] == to, 1.0, 0.0) for k in range(slots)] for to, _ in hops
    ]

    def face_copy(phase, e):
        return pltpu.make_async_remote_copy(
            src_ref=face_out.at[phase, e],
            dst_ref=face_in.at[phase, e],
            send_sem=face_ss.at[phase, e],
            recv_sem=face_rs.at[phase, e],
            device_id={"sub": hops[e][0]},
            device_id_type=MESH,
        )

    def faces_start(phase):
        for k in range(slots):
            packed_ref[k] = pack(local_ref[:, k * depth : (k + 1) * depth])
        for e in reversed(range(len(hops))):
            total = weights[e][0] * packed_ref[0]
            for k in range(1, slots):
                total = total + weights[e][k] * packed_ref[k]
            face_out[phase, e] = total
            face_copy(phase, e).start()

    def faces_end(phase, out_ref):
        for e in range(len(hops)):
            face_copy(phase, e).wait()
        for k in range(0, slots, 2):
            pair = []
            for j in (k, k + 1):
                total = weights[1][j] * face_in[phase, 0]
                for e in range(1, len(hops)):
                    total = total + weights[e ^ 1][j] * face_in[phase, e]
                pair.append(unpack(total, cases, depth))
            at = slice(k * depth, (k + 2) * depth)
            out_ref[:, at] = mask_ref[0:1, at] * (
                local_ref[:, at] + jnp.concatenate(pair, axis=1)
            )

    line = lax.broadcasted_iota(jnp.int32, (cases, 2 * cases), 1)
    case = lax.broadcasted_iota(jnp.int32, (cases, 2 * cases), 0)

    def dots_start(phase, first, second):
        spread = jnp.where(line == case, first, 0.0) + jnp.where(
            line == case + cases, second, 0.0
        )
        total = jnp.sum(spread, axis=0, keepdims=True)
        du_out[phase] = jnp.broadcast_to(total, du_out.shape[1:])
        du_in[phase, sub] = du_out[phase]
        start("sub", lambda p: du_out.at[phase], du_in.at[phase], du_ss.at[phase], du_rs.at[phase])

    def dots_turn(phase):
        receive(
            "sub", lambda p: du_out.at[phase], du_in.at[phase], du_ss.at[phase], du_rs.at[phase]
        )
        dv_out[phase] = jnp.sum(du_in[phase], axis=0)
        dv_in[phase, agg] = dv_out[phase]
        start("agg", lambda p: dv_out.at[phase], dv_in.at[phase], dv_ss.at[phase], dv_rs.at[phase])

    def dots_end(phase):
        receive(
            "agg", lambda p: dv_out.at[phase], dv_in.at[phase], dv_ss.at[phase], dv_rs.at[phase]
        )
        total = jnp.sum(dv_in[phase], axis=0)[0:1]
        first = jnp.sum(jnp.where(line == case, total, 0.0), axis=1, keepdims=True)
        second = jnp.sum(jnp.where(line == case + cases, total, 0.0), axis=1, keepdims=True)
        return first, second

    step = 2 * depth

    def product(vector, matrix, low, high):
        @pl.loop(low, high)
        def _(c):
            at = pl.ds(pl.multiple_of(c * step, 128), step)
            local_ref[:, at] = dot(vector, matrix[:, at]) * mask_ref[0:1, at]

    chunks = order // step

    local_ref[...] = mask * dual_ref[...]
    pl.semaphore_wait(barrier, ns - 1 + na - 1)
    faces_start(0)

    across = lax.broadcasted_iota(jnp.int32, (primal, primal), 1)
    down = lax.broadcasted_iota(jnp.int32, (primal, primal), 0)
    owner_row = jnp.sum(
        jnp.where(across == down, owners_ref[...].astype(F32), 0.0), axis=0, keepdims=True
    )
    hot = jnp.where(
        lax.broadcasted_iota(jnp.int32, (8 * pl.cdiv(na, 8), primal), 0)
        == owner_row.astype(jnp.int32),
        1.0,
        0.0,
    )
    before = jnp.where(down < across, 1.0, 0.0).astype(BF16)
    earlier = dot(hot.astype(BF16), before)
    rank = jnp.sum(hot * earlier, axis=0, keepdims=True)
    late = rank >= half
    place_row = (
        owner_row * half + rank + jnp.where(late, float(used - half), 0.0)
    ).astype(jnp.int32)
    place_hot = jnp.where(
        lax.broadcasted_iota(jnp.int32, (2 * used, primal), 0) == place_row, 1.0, 0.0
    )
    place_col = jnp.sum(
        jnp.where(across == down, place_row.astype(F32), 0.0), axis=1, keepdims=True
    ).astype(jnp.int32)
    value_col = jnp.sum(
        jnp.where(across == down, rows_ref[...].astype(F32) + 1.0, 0.0), axis=1, keepdims=True
    )
    spot = lax.broadcasted_iota(jnp.int32, (primal, wide), 1) - agg * half
    fits = (spot >= 0) & (spot < half)
    tile_row = lax.broadcasted_iota(jnp.int32, (8, wide), 0)
    for o in range(na):
        tile = jnp.zeros((8, wide), F32)
        for h in range(2):
            match = fits & (place_col == spot + (h * used + o * half))
            ids = jnp.sum(jnp.where(match, value_col, 0.0), axis=0, keepdims=True)
            tile = tile + jnp.where(tile_row == h, ids, 0.0)
        ida_out[o] = tile
    ida_in[agg] = ida_out[agg]
    start("agg", lambda p: ida_out.at[p], ida_in, ida_ss, ida_rs)
    cp_ref[...] = dot(place_hot.astype(BF16), coupling_ref[...]).astype(BF16)
    b_in[...] = jnp.zeros_like(b_in)
    receive("agg", lambda p: ida_out.at[p], ida_in, ida_ss, ida_rs)
    mine = jnp.sum(ida_in[...], axis=0)
    idb_out[...] = mine
    idb_in[sub] = mine
    start("sub", lambda p: idb_out, idb_in, idb_ss, idb_rs)

    faces_end(0, residual_ref)

    load_d.wait()
    product(residual_ref[...].astype(BF16), dirichlet_ref, 0, chunks)
    rz = 2.0 * jnp.sum(residual_ref[...] * local_ref[...], axis=1, keepdims=True)
    faces_start(1)

    receive("sub", lambda p: idb_out, idb_in, idb_ss, idb_rs)
    coarse = coarse_ref[...]
    coarse_hi = coarse.astype(BF16)
    coarse_lo = (coarse - coarse_hi.astype(F32)).astype(BF16)
    both = jnp.concatenate([coarse_hi, coarse_lo], axis=0)
    index = lax.broadcasted_iota(jnp.int32, (nc, wide), 0).astype(F32) + 1.0

    @pl.loop(0, ns)
    def _(i):
        for h in range(2):
            chosen = jnp.where(index == idb_in[i, h : h + 1, :], 1.0, 0.0).astype(BF16)
            spread = dot(both, chosen).astype(BF16)
            at = pl.ds(pl.multiple_of(i * wide, 128), wide)
            hi_ref[h * crow : (h + 1) * crow, at] = spread[:crow]
            lo_ref[h * crow : (h + 1) * crow, at] = spread[crow:]

    fold = crow // 2
    held = ns * fold
    square = lax.broadcasted_iota(jnp.int32, (wide, wide), 0) == lax.broadcasted_iota(
        jnp.int32, (wide, wide), 1
    )
    at_lane = lax.broadcasted_iota(jnp.int32, (used, held), 1)
    number = (at_lane // fold) * crow + at_lane % fold + 1
    for h in range(2):
        ids = idb_out[h : h + 1, :]
        column = jnp.sum(jnp.where(square, ids, 0.0), axis=1, keepdims=True)
        column = column[:used].astype(jnp.int32)
        for g in range(2):
            found = jnp.where(number + g * fold == column, 1.0, 0.0)
            pick_ref[(2 * h + g) * used : (2 * h + g + 1) * used, :] = found.astype(BF16)

    faces_end(1, direction_ref)
    load_k.wait()

    for it in range(ITERS):
        vector = direction_ref[...].astype(BF16)
        terms = lax.dot_general(cp_ref[...], vector, NT, preferred_element_type=F32)
        out = jnp.concatenate([terms[:used], terms[used:]], axis=1)
        a_out[it] = out.reshape(na, half, 2 * cases)
        a_in[it, agg] = a_out[it, agg]
        start("agg", lambda p: a_out.at[it, p], a_in.at[it], a_ss.at[it], a_rs.at[it])
        product(vector, inverse_ref, 0, chunks // 2)
        receive("agg", lambda p: a_out.at[it, p], a_in.at[it], a_ss.at[it], a_rs.at[it])
        b_out[it] = a_in[it].reshape(used, 2 * cases)
        b_in[it, sub, 0:used] = b_out[it]

        def b_dst(j):
            return b_in.at[it, j, pl.ds(0, used)]

        @pl.loop(1, ns)
        def _(t):
            peer = lax.rem(sub + t, ns)
            pltpu.make_async_remote_copy(
                src_ref=b_out.at[it],
                dst_ref=b_dst(sub),
                send_sem=b_ss.at[it, t - 1],
                recv_sem=b_rs.at[it, t - 1],
                device_id={"sub": peer},
                device_id_type=MESH,
            ).start()

        product(vector, inverse_ref, chunks // 2, chunks)

        @pl.loop(1, ns)
        def _(t):
            peer = lax.rem(sub - t + ns, ns)
            copy = pltpu.make_async_remote_copy(
                src_ref=b_out.at[it],
                dst_ref=b_dst(peer),
                send_sem=b_ss.at[it, t - 1],
                recv_sem=b_rs.at[it, t - 1],
                device_id={"sub": peer},
                device_id_type=MESH,
            )
            copy.wait_recv()
            copy.wait_send()

        given = b_in[it].reshape(ns * wide, 2 * cases)
        given_hi = given.astype(BF16)
        given_lo = (given - given_hi.astype(F32)).astype(BF16)
        solved = (
            dot(hi_ref[...], given_hi) + dot(hi_ref[...], given_lo) + dot(lo_ref[...], given_hi)
        )
        rows = solved[:crow, :cases] + solved[crow:, cases:]
        s_out[it] = jnp.concatenate([rows[:fold], rows[fold:]], axis=1)
        s_in[it, sub] = s_out[it]
        start("sub", lambda p: s_out.at[it], s_in.at[it], s_ss.at[it], s_rs.at[it])
        receive("sub", lambda p: s_out.at[it], s_in.at[it], s_ss.at[it], s_rs.at[it])
        found = dot(pick_ref[...], s_in[it].reshape(held, 2 * cases).astype(BF16))
        answer = jnp.concatenate(
            [
                found[2 * h * used : (2 * h + 1) * used, :cases]
                + found[(2 * h + 1) * used : (2 * h + 2) * used, cases:]
                for h in range(2)
            ],
            axis=1,
        )
        r_out[it] = answer.reshape(na, half, 2 * cases)
        r_in[it, agg] = r_out[it, agg]
        start("agg", lambda p: r_out.at[it, p], r_in.at[it], r_ss.at[it], r_rs.at[it])
        receive("agg", lambda p: r_out.at[it, p], r_in.at[it], r_ss.at[it], r_rs.at[it])
        came = r_in[it].reshape(used, 2 * cases)
        back = jnp.concatenate([came[:, :cases], came[:, cases:]], axis=0)
        back = jnp.transpose(back).astype(BF16)

        @pl.loop(0, chunks)
        def _(c):
            at = pl.ds(pl.multiple_of(c * step, 128), step)
            local_ref[:, at] += dot(back, cp_ref[:, at]) * mask_ref[0:1, at]

        image_dot = 2.0 * jnp.sum(direction_ref[...] * local_ref[...], axis=1, keepdims=True)
        phase = 2 * it
        dots_start(phase, rz, image_dot)
        faces_start(2 + phase)
        dots_turn(phase)
        faces_end(2 + phase, field_ref)
        first, second = dots_end(phase)
        if it == 0:
            rz = first
        else:
            rz = rz_all
        alpha = rz / second
        if it == 0:
            solution_ref[...] = alpha * direction_ref[...]
        else:
            solution_ref[...] += alpha * direction_ref[...]
        residual_ref[...] -= alpha * field_ref[...]
        if it + 1 < ITERS:
            product(residual_ref[...].astype(BF16), dirichlet_ref, 0, chunks)
            part = 2.0 * jnp.sum(residual_ref[...] * local_ref[...], axis=1, keepdims=True)
            dots_start(phase + 1, part, part)
            faces_start(3 + phase)
            dots_turn(phase + 1)
            faces_end(3 + phase, field_ref)
            rz_all = dots_end(phase + 1)[0]
            direction_ref[...] = field_ref[...] + (rz_all / rz) * direction_ref[...]


def shards(
    dual_load,
    interface_inverse,
    dirichlet,
    coupling,
    neighbours,
    face_counts,
    owners,
    primal_rows,
    coarse_inverse,
):
    ns = lax.axis_size("sub")
    na = lax.axis_size("agg")
    reach = min(4, (ns - 1) // 2)
    cases, order = dual_load.shape[2:]
    slots = neighbours.shape[2]
    depth = order // slots
    crow, nc = coarse_inverse.shape[1:]
    half = CAP // 2
    used = na * half
    wide = pl.cdiv(used, 128) * 128
    lanes = 2 * cases
    face_rows = cases * depth // 128
    phases = 2 * ITERS + 1
    dots = 2 * ITERS - 1
    dma = pltpu.SemaphoreType.DMA

    def exchange(times, n, out, rows):
        return [
            pltpu.VMEM(out, F32),
            pltpu.VMEM(rows, F32),
            dma((times, n - 1) if times else (n - 1,)),
            dma((times, n - 1) if times else (n - 1,)),
        ]

    scratch = [
        pltpu.VMEM((order, order), BF16),
        pltpu.VMEM((order, order), BF16),
        pltpu.VMEM((cases, order), F32),
        pltpu.VMEM((cases, order), F32),
        pltpu.VMEM((cases, order), F32),
        pltpu.VMEM((slots, face_rows, 128), F32),
        pltpu.VMEM((phases, 2 * reach, face_rows, 128), F32),
        pltpu.VMEM((phases, 2 * reach, face_rows, 128), F32),
        dma((phases, 2 * reach)),
        dma((phases, 2 * reach)),
        dma((2,)),
        pltpu.VMEM((2 * used, order), BF16),
        pltpu.VMEM((8, order), F32),
        *exchange(0, na, (na, 8, wide), (na, 8, wide)),
        *exchange(0, ns, (8, wide), (ns, 8, wide)),
        pltpu.VMEM((2 * crow, ns * wide), BF16),
        pltpu.VMEM((2 * crow, ns * wide), BF16),
        pltpu.VMEM((4 * used, ns * crow // 2), BF16),
        *exchange(ITERS, na, (ITERS, na, half, lanes), (ITERS, na, half, lanes)),
        *exchange(ITERS, ns, (ITERS, used, lanes), (ITERS, ns, wide, lanes)),
        *exchange(ITERS, ns, (ITERS, crow // 2, lanes), (ITERS, ns, crow // 2, lanes)),
        *exchange(ITERS, na, (ITERS, na, half, lanes), (ITERS, na, half, lanes)),
        *exchange(dots, ns, (dots, 8, lanes), (dots, ns, 8, lanes)),
        *exchange(dots, na, (dots, 8, lanes), (dots, na, 8, lanes)),
    ]
    vmem = pl.BlockSpec(memory_space=pltpu.VMEM)
    smem = pl.BlockSpec(memory_space=pltpu.SMEM)
    anywhere = pl.BlockSpec(memory_space=pl.ANY)
    shape = jax.ShapeDtypeStruct((cases, order), F32)
    solved, left = pl.pallas_call(
        functools.partial(kernel, ns, na, reach),
        out_shape=(shape, shape),
        in_specs=[vmem, anywhere, anywhere, vmem, smem, smem, vmem, vmem, vmem],
        out_specs=(vmem, vmem),
        scratch_shapes=scratch,
        compiler_params=pltpu.CompilerParams(
            collective_id=0, has_side_effects=True, vmem_limit_bytes=56 * 1024 * 1024
        ),
    )(
        dual_load[0, 0],
        interface_inverse[0, 0],
        dirichlet[0, 0],
        coupling[0, 0],
        neighbours[0, 0],
        face_counts[0, 0],
        owners[0, 0],
        primal_rows[0],
        coarse_inverse[0],
    )
    return solved[None, None], left[None, None]


def solution(mesh):
    in_specs = (
        P("agg", "sub", None, None),
        P("agg", "sub", None, None),
        P("agg", "sub", None, None),
        P("agg", "sub", None, None),
        P("agg", "sub", None),
        P("agg", "sub", None),
        P("agg", "sub", None, None),
        P("agg", "sub", None),
        P("agg", "sub", None),
    )
    out_specs = (P("agg", "sub", None, None), P("agg", "sub", None, None))
    return jax.shard_map(shards, mesh=mesh, in_specs=in_specs, out_specs=out_specs, check_vma=False)
```

```python
import functools

import jax
import jax.numpy as jnp
from jax import lax
from jax.experimental import pallas as pl
from jax.experimental.pallas import tpu as pltpu
from jax.sharding import PartitionSpec as P

CAP = 48
ITERS = 2
MESH = pl.DeviceIdType.MESH
F32 = jnp.float32
BF16 = jnp.bfloat16
NT = (((1,), (1,)), ((), ()))


def dot(left, right):
    return jnp.dot(left, right, preferred_element_type=F32)


def pack(face):
    cases, depth = face.shape
    whole = depth // 128 * 128
    half = cases // 2
    parts = [face[:, at : at + 128] for at in range(0, whole, 128)]
    if depth > whole:
        parts.append(jnp.concatenate([face[:half, whole:], face[half:, whole:]], axis=1))
    return jnp.concatenate(parts, axis=0)


def unpack(rows, cases, depth):
    whole = depth // 128 * 128
    parts = [rows[at * cases : (at + 1) * cases] for at in range(whole // 128)]
    if depth > whole:
        last = rows[whole // 128 * cases :]
        wide = depth - whole
        parts.append(jnp.concatenate([last[:, :wide], last[:, wide:]], axis=0))
    return jnp.concatenate(parts, axis=1)


def kernel(
    ns,
    na,
    reach,
    dual_ref,
    inverse_hbm,
    dirichlet_hbm,
    coupling_ref,
    peers_ref,
    counts_ref,
    owners_ref,
    rows_ref,
    coarse_ref,
    solution_ref,
    residual_ref,
    inverse_ref,
    dirichlet_ref,
    local_ref,
    field_ref,
    direction_ref,
    packed_ref,
    face_out,
    face_in,
    face_ss,
    face_rs,
    load_sem,
    cp_ref,
    mask_ref,
    ida_out,
    ida_in,
    ida_ss,
    ida_rs,
    idb_out,
    idb_in,
    idb_ss,
    idb_rs,
    hi_ref,
    lo_ref,
    pick_ref,
    a_out,
    a_in,
    a_ss,
    a_rs,
    b_out,
    b_in,
    b_ss,
    b_rs,
    s_out,
    s_in,
    s_ss,
    s_rs,
    r_out,
    r_in,
    r_ss,
    r_rs,
    du_out,
    du_in,
    du_ss,
    du_rs,
    dv_out,
    dv_in,
    dv_ss,
    dv_rs,
):
    cases, order = dual_ref.shape
    slots = peers_ref.shape[0]
    depth = order // slots
    primal = coupling_ref.shape[0]
    crow, nc = coarse_ref.shape
    half = CAP // 2
    used = na * half
    wide = ida_in.shape[2]
    sub = lax.axis_index("sub")
    agg = lax.axis_index("agg")

    def start(axis, src_of, dst, ss, rs):
        me, n = (sub, ns) if axis == "sub" else (agg, na)

        @pl.loop(1, n)
        def _(t):
            peer = lax.rem(me + t, n)
            pltpu.make_async_remote_copy(
                src_ref=src_of(peer),
                dst_ref=dst.at[me],
                send_sem=ss.at[t - 1],
                recv_sem=rs.at[t - 1],
                device_id={axis: peer},
                device_id_type=MESH,
            ).start()

    def receive(axis, src_of, dst, ss, rs):
        me, n = (sub, ns) if axis == "sub" else (agg, na)

        @pl.loop(1, n)
        def _(t):
            peer = lax.rem(me - t + n, n)
            copy = pltpu.make_async_remote_copy(
                src_ref=src_of(peer),
                dst_ref=dst.at[peer],
                send_sem=ss.at[t - 1],
                recv_sem=rs.at[t - 1],
                device_id={axis: peer},
                device_id_type=MESH,
            )
            copy.wait_recv()
            copy.wait_send()

    pairs = ns // 2
    pair, parity = lax.div(sub, 2), lax.rem(sub, 2)

    def ahead_of(t):
        return 2 * lax.rem(pair + t, pairs) + parity

    def behind(t, side):
        return 2 * lax.rem(pair - t + pairs, pairs) + side

    def leg(src, dst, k, ss, rs, to):
        return pltpu.make_async_remote_copy(
            src_ref=src,
            dst_ref=dst,
            send_sem=ss.at[k],
            recv_sem=rs.at[k],
            device_id={"sub": to},
            device_id_type=MESH,
        )

    partner = 2 * pair + 1 - parity

    def spread_start(src, dst_of, ss, rs):
        @pl.loop(1, pairs)
        def _(t):
            leg(src, dst_of(sub), t - 1, ss, rs, ahead_of(t)).start()

        leg(src, dst_of(sub), pairs - 1, ss, rs, partner).start()

    def spread_end(src, dst_of, ss, rs):
        @pl.loop(1, pairs)
        def _(t):
            block = dst_of(behind(t, parity))
            leg(src, block, t - 1, ss, rs, ahead_of(t)).wait_recv()
            leg(block, block, pairs - 1 + t, ss, rs, partner).start()

        leg(src, dst_of(partner), pairs - 1, ss, rs, partner).wait_recv()

        @pl.loop(1, pairs)
        def _(t):
            block = dst_of(behind(t, 1 - parity))
            leg(src, block, pairs - 1 + t, ss, rs, partner).wait_recv()

        @pl.loop(0, 2 * pairs - 1)
        def _(k):
            leg(src, dst_of(sub), k, ss, rs, partner).wait_send()

    barrier = pltpu.get_barrier_semaphore()
    for axis, me, n in (("sub", sub, ns), ("agg", agg, na)):

        @pl.loop(1, n)
        def _(t, axis=axis, me=me, n=n):
            pl.semaphore_signal(
                barrier, inc=1, device_id={axis: lax.rem(me + t, n)}, device_id_type=MESH
            )

    load_d = pltpu.make_async_copy(dirichlet_hbm, dirichlet_ref, load_sem.at[0])
    load_k = pltpu.make_async_copy(inverse_hbm, inverse_ref, load_sem.at[1])
    load_d.start()
    load_k.start()

    lane = lax.broadcasted_iota(jnp.int32, (1, order), 1)
    mask = jnp.zeros((1, order), F32)
    for k in range(slots):
        inside = (lane >= k * depth) & (lane < k * depth + counts_ref[k])
        mask = mask + jnp.where(inside, 1.0, 0.0)
    mask_ref[...] = jnp.broadcast_to(mask, mask_ref.shape)

    hops = []
    for distance in range(1, reach + 1):
        ahead = lax.rem(sub + distance, ns)
        back = lax.rem(sub + ns - distance, ns)
        hops.append((ahead, back))
        hops.append((back, ahead))
    weights = [
        [jnp.where(peers_ref[k] == to, 1.0, 0.0) for k in range(slots)] for to, _ in hops
    ]

    def face_copy(phase, e):
        return pltpu.make_async_remote_copy(
            src_ref=face_out.at[phase, e],
            dst_ref=face_in.at[phase, e],
            send_sem=face_ss.at[phase, e],
            recv_sem=face_rs.at[phase, e],
            device_id={"sub": hops[e][0]},
            device_id_type=MESH,
        )

    def faces_start(phase):
        for k in range(slots):
            packed_ref[k] = pack(local_ref[:, k * depth : (k + 1) * depth])
        for e in reversed(range(len(hops))):
            total = weights[e][0] * packed_ref[0]
            for k in range(1, slots):
                total = total + weights[e][k] * packed_ref[k]
            face_out[phase, e] = total
            face_copy(phase, e).start()

    def faces_end(phase, out_ref):
        for e in range(len(hops)):
            face_copy(phase, e).wait()
        for k in range(0, slots, 2):
            pair = []
            for j in (k, k + 1):
                total = weights[1][j] * face_in[phase, 0]
                for e in range(1, len(hops)):
                    total = total + weights[e ^ 1][j] * face_in[phase, e]
                pair.append(unpack(total, cases, depth))
            at = slice(k * depth, (k + 2) * depth)
            out_ref[:, at] = mask_ref[0:1, at] * (
                local_ref[:, at] + jnp.concatenate(pair, axis=1)
            )

    line = lax.broadcasted_iota(jnp.int32, (cases, 2 * cases), 1)
    case = lax.broadcasted_iota(jnp.int32, (cases, 2 * cases), 0)

    def dots_start(phase, first, second):
        spread = jnp.where(line == case, first, 0.0) + jnp.where(
            line == case + cases, second, 0.0
        )
        total = jnp.sum(spread, axis=0, keepdims=True)
        du_out[phase] = jnp.broadcast_to(total, du_out.shape[1:])
        du_in[phase, sub] = du_out[phase]
        start("sub", lambda p: du_out.at[phase], du_in.at[phase], du_ss.at[phase], du_rs.at[phase])

    def dots_turn(phase):
        receive(
            "sub", lambda p: du_out.at[phase], du_in.at[phase], du_ss.at[phase], du_rs.at[phase]
        )
        dv_out[phase] = jnp.sum(du_in[phase], axis=0)
        dv_in[phase, agg] = dv_out[phase]
        start("agg", lambda p: dv_out.at[phase], dv_in.at[phase], dv_ss.at[phase], dv_rs.at[phase])

    def dots_end(phase):
        receive(
            "agg", lambda p: dv_out.at[phase], dv_in.at[phase], dv_ss.at[phase], dv_rs.at[phase]
        )
        total = jnp.sum(dv_in[phase], axis=0)[0:1]
        first = jnp.sum(jnp.where(line == case, total, 0.0), axis=1, keepdims=True)
        second = jnp.sum(jnp.where(line == case + cases, total, 0.0), axis=1, keepdims=True)
        return first, second

    step = next(w for w in (512, 384, 256, 128, order) if order % w == 0)

    def product(vector, matrix, low, high):
        @pl.loop(low, high)
        def _(c):
            at = pl.ds(pl.multiple_of(c * step, 128), step)
            local_ref[:, at] = dot(vector, matrix[:, at]) * mask_ref[0:1, at]

    chunks = order // step

    local_ref[...] = mask * dual_ref[...]
    pl.semaphore_wait(barrier, ns - 1 + na - 1)
    faces_start(0)

    across = lax.broadcasted_iota(jnp.int32, (primal, primal), 1)
    down = lax.broadcasted_iota(jnp.int32, (primal, primal), 0)
    owner_row = owners_ref[...].astype(F32)
    hot = jnp.where(
        lax.broadcasted_iota(jnp.int32, (8 * pl.cdiv(na, 8), primal), 0)
        == owner_row.astype(jnp.int32),
        1.0,
        0.0,
    )
    before = jnp.where(down < across, 1.0, 0.0).astype(BF16)
    earlier = dot(hot.astype(BF16), before)
    rank = jnp.sum(hot * earlier, axis=0, keepdims=True)
    late = rank >= half
    place_row = (
        owner_row * half + rank + jnp.where(late, float(used - half), 0.0)
    ).astype(jnp.int32)
    place_hot = jnp.where(
        lax.broadcasted_iota(jnp.int32, (2 * used, primal), 0) == place_row, 1.0, 0.0
    )
    place_col = jnp.sum(
        jnp.where(across == down, place_row.astype(F32), 0.0), axis=1, keepdims=True
    ).astype(jnp.int32)
    value_col = jnp.sum(
        jnp.where(across == down, rows_ref[...].astype(F32) + 1.0, 0.0), axis=1, keepdims=True
    )
    spot = lax.broadcasted_iota(jnp.int32, (primal, wide), 1) - agg * half
    fits = (spot >= 0) & (spot < half)
    tile_row = lax.broadcasted_iota(jnp.int32, (8, wide), 0)
    for o in range(na):
        tile = jnp.zeros((8, wide), F32)
        for h in range(2):
            match = fits & (place_col == spot + (h * used + o * half))
            ids = jnp.sum(jnp.where(match, value_col, 0.0), axis=0, keepdims=True)
            tile = tile + jnp.where(tile_row == h, ids, 0.0)
        ida_out[o] = tile
    ida_in[agg] = ida_out[agg]
    start("agg", lambda p: ida_out.at[p], ida_in, ida_ss, ida_rs)
    cp_ref[...] = dot(place_hot.astype(BF16), coupling_ref[...]).astype(BF16)
    b_in[...] = jnp.zeros_like(b_in)
    receive("agg", lambda p: ida_out.at[p], ida_in, ida_ss, ida_rs)
    mine = jnp.sum(ida_in[...], axis=0)
    idb_out[...] = mine
    idb_in[sub] = mine
    start("sub", lambda p: idb_out, idb_in, idb_ss, idb_rs)

    faces_end(0, residual_ref)

    load_d.wait()
    product(residual_ref[...].astype(BF16), dirichlet_ref, 0, chunks)
    rz = 2.0 * jnp.sum(residual_ref[...] * local_ref[...], axis=1, keepdims=True)
    faces_start(1)

    receive("sub", lambda p: idb_out, idb_in, idb_ss, idb_rs)
    coarse = coarse_ref[...]
    coarse_hi = coarse.astype(BF16)
    coarse_lo = (coarse - coarse_hi.astype(F32)).astype(BF16)
    both = jnp.concatenate([coarse_hi, coarse_lo], axis=0)
    index = lax.broadcasted_iota(jnp.int32, (nc, wide), 0).astype(F32) + 1.0

    @pl.loop(0, ns)
    def _(i):
        chosen = jnp.concatenate(
            [
                jnp.where(index == idb_in[i, h : h + 1, :], 1.0, 0.0).astype(BF16)
                for h in range(2)
            ],
            axis=1,
        )
        spread = dot(both, chosen).astype(BF16)
        at = pl.ds(pl.multiple_of(i * wide, 128), wide)
        for h in range(2):
            part = spread[:, h * wide : (h + 1) * wide]
            hi_ref[h * crow : (h + 1) * crow, at] = part[:crow]
            lo_ref[h * crow : (h + 1) * crow, at] = part[crow:]

    fold = crow // 2
    held = ns * fold
    square = lax.broadcasted_iota(jnp.int32, (wide, wide), 0) == lax.broadcasted_iota(
        jnp.int32, (wide, wide), 1
    )
    at_lane = lax.broadcasted_iota(jnp.int32, (used, held), 1)
    number = (at_lane // fold) * crow + at_lane % fold + 1
    for h in range(2):
        ids = idb_out[h : h + 1, :]
        column = jnp.sum(jnp.where(square, ids, 0.0), axis=1, keepdims=True)
        column = column[:used].astype(jnp.int32)
        for g in range(2):
            found = jnp.where(number + g * fold == column, 1.0, 0.0)
            pick_ref[(2 * h + g) * used : (2 * h + g + 1) * used, :] = found.astype(BF16)

    faces_end(1, direction_ref)
    load_k.wait()

    for it in range(ITERS):
        vector = direction_ref[...].astype(BF16)
        terms = lax.dot_general(cp_ref[...], vector, NT, preferred_element_type=F32)
        out = jnp.concatenate([terms[:used], terms[used:]], axis=1)
        a_out[it] = out.reshape(na, half, 2 * cases)
        a_in[it, agg] = a_out[it, agg]
        start("agg", lambda p: a_out.at[it, p], a_in.at[it], a_ss.at[it], a_rs.at[it])
        product(vector, inverse_ref, 0, chunks // 2)
        receive("agg", lambda p: a_out.at[it, p], a_in.at[it], a_ss.at[it], a_rs.at[it])
        b_out[it] = a_in[it].reshape(used, 2 * cases)
        b_in[it, sub, 0:used] = b_out[it]

        def b_dst(j):
            return b_in.at[it, j, pl.ds(0, used)]

        spread_start(b_out.at[it], b_dst, b_ss.at[it], b_rs.at[it])
        product(vector, inverse_ref, chunks // 2, chunks)

        spread_end(b_out.at[it], b_dst, b_ss.at[it], b_rs.at[it])
        given = b_in[it].reshape(ns * wide, 2 * cases)
        given_hi = given.astype(BF16)
        given_lo = (given - given_hi.astype(F32)).astype(BF16)
        solved = (
            dot(hi_ref[...], given_hi) + dot(hi_ref[...], given_lo) + dot(lo_ref[...], given_hi)
        )
        rows = solved[:crow, :cases] + solved[crow:, cases:]
        s_out[it] = jnp.concatenate([rows[:fold], rows[fold:]], axis=1)
        s_in[it, sub] = s_out[it]

        def s_dst(j):
            return s_in.at[it, j]

        spread_start(s_out.at[it], s_dst, s_ss.at[it], s_rs.at[it])
        spread_end(s_out.at[it], s_dst, s_ss.at[it], s_rs.at[it])
        found = dot(pick_ref[...], s_in[it].reshape(held, 2 * cases).astype(BF16))
        answer = jnp.concatenate(
            [
                found[2 * h * used : (2 * h + 1) * used, :cases]
                + found[(2 * h + 1) * used : (2 * h + 2) * used, cases:]
                for h in range(2)
            ],
            axis=1,
        )
        r_out[it] = answer.reshape(na, half, 2 * cases)
        r_in[it, agg] = r_out[it, agg]
        start("agg", lambda p: r_out.at[it, p], r_in.at[it], r_ss.at[it], r_rs.at[it])
        receive("agg", lambda p: r_out.at[it, p], r_in.at[it], r_ss.at[it], r_rs.at[it])
        came = r_in[it].reshape(used, 2 * cases)
        back = jnp.concatenate([came[:, :cases], came[:, cases:]], axis=0)
        back = jnp.transpose(back).astype(BF16)

        @pl.loop(0, chunks)
        def _(c):
            at = pl.ds(pl.multiple_of(c * step, 128), step)
            local_ref[:, at] += dot(back, cp_ref[:, at]) * mask_ref[0:1, at]

        image_dot = 2.0 * jnp.sum(direction_ref[...] * local_ref[...], axis=1, keepdims=True)
        phase = 2 * it
        dots_start(phase, rz, image_dot)
        faces_start(2 + phase)
        dots_turn(phase)
        faces_end(2 + phase, field_ref)
        first, second = dots_end(phase)
        if it == 0:
            rz = first
        else:
            rz = rz_all
        alpha = rz / second
        if it == 0:
            solution_ref[...] = alpha * direction_ref[...]
        else:
            solution_ref[...] += alpha * direction_ref[...]
        residual_ref[...] -= alpha * field_ref[...]
        if it + 1 < ITERS:
            product(residual_ref[...].astype(BF16), dirichlet_ref, 0, chunks)
            part = 2.0 * jnp.sum(residual_ref[...] * local_ref[...], axis=1, keepdims=True)
            dots_start(phase + 1, part, part)
            faces_start(3 + phase)
            dots_turn(phase + 1)
            faces_end(3 + phase, field_ref)
            rz_all = dots_end(phase + 1)[0]
            direction_ref[...] = field_ref[...] + (rz_all / rz) * direction_ref[...]


def shards(
    dual_load,
    interface_inverse,
    dirichlet,
    coupling,
    neighbours,
    face_counts,
    owners,
    primal_rows,
    coarse_inverse,
):
    ns = lax.axis_size("sub")
    na = lax.axis_size("agg")
    reach = min(4, (ns - 1) // 2)
    cases, order = dual_load.shape[2:]
    slots = neighbours.shape[2]
    depth = order // slots
    crow, nc = coarse_inverse.shape[1:]
    half = CAP // 2
    used = na * half
    wide = pl.cdiv(used, 128) * 128
    lanes = 2 * cases
    face_rows = cases * depth // 128
    phases = 2 * ITERS + 1
    dots = 2 * ITERS - 1
    dma = pltpu.SemaphoreType.DMA

    def exchange(times, n, out, rows):
        return [
            pltpu.VMEM(out, F32),
            pltpu.VMEM(rows, F32),
            dma((times, n - 1) if times else (n - 1,)),
            dma((times, n - 1) if times else (n - 1,)),
        ]

    scratch = [
        pltpu.VMEM((order, order), BF16),
        pltpu.VMEM((order, order), BF16),
        pltpu.VMEM((cases, order), F32),
        pltpu.VMEM((cases, order), F32),
        pltpu.VMEM((cases, order), F32),
        pltpu.VMEM((slots, face_rows, 128), F32),
        pltpu.VMEM((phases, 2 * reach, face_rows, 128), F32),
        pltpu.VMEM((phases, 2 * reach, face_rows, 128), F32),
        dma((phases, 2 * reach)),
        dma((phases, 2 * reach)),
        dma((2,)),
        pltpu.VMEM((2 * used, order), BF16),
        pltpu.VMEM((8, order), F32),
        *exchange(0, na, (na, 8, wide), (na, 8, wide)),
        *exchange(0, ns, (8, wide), (ns, 8, wide)),
        pltpu.VMEM((2 * crow, ns * wide), BF16),
        pltpu.VMEM((2 * crow, ns * wide), BF16),
        pltpu.VMEM((4 * used, ns * crow // 2), BF16),
        *exchange(ITERS, na, (ITERS, na, half, lanes), (ITERS, na, half, lanes)),
        *exchange(ITERS, ns, (ITERS, used, lanes), (ITERS, ns, wide, lanes)),
        *exchange(ITERS, ns, (ITERS, crow // 2, lanes), (ITERS, ns, crow // 2, lanes)),
        *exchange(ITERS, na, (ITERS, na, half, lanes), (ITERS, na, half, lanes)),
        *exchange(dots, ns, (dots, 8, lanes), (dots, ns, 8, lanes)),
        *exchange(dots, na, (dots, 8, lanes), (dots, na, 8, lanes)),
    ]
    vmem = pl.BlockSpec(memory_space=pltpu.VMEM)
    smem = pl.BlockSpec(memory_space=pltpu.SMEM)
    anywhere = pl.BlockSpec(memory_space=pl.ANY)
    shape = jax.ShapeDtypeStruct((cases, order), F32)
    solved, left = pl.pallas_call(
        functools.partial(kernel, ns, na, reach),
        out_shape=(shape, shape),
        in_specs=[vmem, anywhere, anywhere, vmem, smem, smem, vmem, vmem, vmem],
        out_specs=(vmem, vmem),
        scratch_shapes=scratch,
        compiler_params=pltpu.CompilerParams(
            collective_id=0, has_side_effects=True, vmem_limit_bytes=56 * 1024 * 1024
        ),
    )(
        dual_load[0, 0],
        interface_inverse[0, 0],
        dirichlet[0, 0],
        coupling[0, 0],
        neighbours[0, 0],
        face_counts[0, 0],
        owners[0, 0].reshape(1, -1),
        primal_rows[0],
        coarse_inverse[0],
    )
    return solved[None, None], left[None, None]


def solution(mesh):
    in_specs = (
        P("agg", "sub", None, None),
        P("agg", "sub", None, None),
        P("agg", "sub", None, None),
        P("agg", "sub", None, None),
        P("agg", "sub", None),
        P("agg", "sub", None),
        P("agg", "sub", None, None),
        P("agg", "sub", None),
        P("agg", "sub", None),
    )
    out_specs = (P("agg", "sub", None, None), P("agg", "sub", None, None))
    return jax.shard_map(shards, mesh=mesh, in_specs=in_specs, out_specs=out_specs, check_vma=False)
```

```python
import functools

import jax
import jax.numpy as jnp
from jax import lax
from jax.experimental import pallas as pl
from jax.experimental.pallas import tpu as pltpu
from jax.sharding import PartitionSpec as P

CAP = 48
ITERS = 2
MESH = pl.DeviceIdType.MESH
F32 = jnp.float32
BF16 = jnp.bfloat16
NT = (((1,), (1,)), ((), ()))


def dot(left, right):
    return jnp.dot(left, right, preferred_element_type=F32)


def pack(face):
    cases, depth = face.shape
    whole = depth // 128 * 128
    half = cases // 2
    parts = [face[:, at : at + 128] for at in range(0, whole, 128)]
    if depth > whole:
        parts.append(jnp.concatenate([face[:half, whole:], face[half:, whole:]], axis=1))
    return jnp.concatenate(parts, axis=0)


def unpack(rows, cases, depth):
    whole = depth // 128 * 128
    parts = [rows[at * cases : (at + 1) * cases] for at in range(whole // 128)]
    if depth > whole:
        last = rows[whole // 128 * cases :]
        wide = depth - whole
        parts.append(jnp.concatenate([last[:, :wide], last[:, wide:]], axis=0))
    return jnp.concatenate(parts, axis=1)


def kernel(
    ns,
    na,
    reach,
    dual_ref,
    inverse_hbm,
    dirichlet_hbm,
    coupling_ref,
    peers_ref,
    counts_ref,
    owners_ref,
    rows_ref,
    coarse_ref,
    solution_ref,
    residual_ref,
    inverse_ref,
    dirichlet_ref,
    local_ref,
    field_ref,
    direction_ref,
    packed_ref,
    face_out,
    face_in,
    face_ss,
    face_rs,
    load_sem,
    cp_ref,
    mask_ref,
    ida_out,
    ida_in,
    ida_ss,
    ida_rs,
    idb_out,
    idb_in,
    idb_ss,
    idb_rs,
    hi_ref,
    lo_ref,
    pick_ref,
    a_out,
    a_in,
    a_ss,
    a_rs,
    b_out,
    b_in,
    b_ss,
    b_rs,
    s_out,
    s_in,
    s_ss,
    s_rs,
    r_out,
    r_in,
    r_ss,
    r_rs,
    du_out,
    du_in,
    du_ss,
    du_rs,
    dv_out,
    dv_in,
    dv_ss,
    dv_rs,
):
    cases, order = dual_ref.shape
    slots = peers_ref.shape[0]
    depth = order // slots
    primal = coupling_ref.shape[0]
    crow, nc = coarse_ref.shape
    half = CAP // 2
    used = na * half
    wide = ida_in.shape[2]
    sub = lax.axis_index("sub")
    agg = lax.axis_index("agg")

    unsent = []

    def start(axis, src_of, dst, ss, rs):
        me, n = (sub, ns) if axis == "sub" else (agg, na)

        @pl.loop(1, n)
        def _(t):
            peer = lax.rem(me + t, n)
            pltpu.make_async_remote_copy(
                src_ref=src_of(peer),
                dst_ref=dst.at[me],
                send_sem=ss.at[t - 1],
                recv_sem=rs.at[t - 1],
                device_id={axis: peer},
                device_id_type=MESH,
            ).start()

    def receive(axis, src_of, dst, ss, rs):
        me, n = (sub, ns) if axis == "sub" else (agg, na)

        def copy(t):
            peer = lax.rem(me - t + n, n)
            return pltpu.make_async_remote_copy(
                src_ref=src_of(peer),
                dst_ref=dst.at[peer],
                send_sem=ss.at[t - 1],
                recv_sem=rs.at[t - 1],
                device_id={axis: peer},
                device_id_type=MESH,
            )

        @pl.loop(1, n)
        def _(t):
            copy(t).wait_recv()

        def sent():
            @pl.loop(1, n)
            def _(t):
                copy(t).wait_send()

        unsent.append(sent)

    pairs = ns // 2
    pair, parity = lax.div(sub, 2), lax.rem(sub, 2)

    def ahead_of(t):
        return 2 * lax.rem(pair + t, pairs) + parity

    def behind(t, side):
        return 2 * lax.rem(pair - t + pairs, pairs) + side

    def leg(src, dst, k, ss, rs, to):
        return pltpu.make_async_remote_copy(
            src_ref=src,
            dst_ref=dst,
            send_sem=ss.at[k],
            recv_sem=rs.at[k],
            device_id={"sub": to},
            device_id_type=MESH,
        )

    partner = 2 * pair + 1 - parity

    def spread_start(src, dst_of, ss, rs):
        @pl.loop(1, pairs)
        def _(t):
            leg(src, dst_of(sub), t - 1, ss, rs, ahead_of(t)).start()

        leg(src, dst_of(sub), pairs - 1, ss, rs, partner).start()

    def spread_end(src, dst_of, ss, rs):
        @pl.loop(1, pairs)
        def _(t):
            block = dst_of(behind(t, parity))
            leg(src, block, t - 1, ss, rs, ahead_of(t)).wait_recv()
            leg(block, block, pairs - 1 + t, ss, rs, partner).start()

        leg(src, dst_of(partner), pairs - 1, ss, rs, partner).wait_recv()

        @pl.loop(1, pairs)
        def _(t):
            block = dst_of(behind(t, 1 - parity))
            leg(src, block, pairs - 1 + t, ss, rs, partner).wait_recv()

        def sent():
            @pl.loop(0, 2 * pairs - 1)
            def _(k):
                leg(src, dst_of(sub), k, ss, rs, partner).wait_send()

        unsent.append(sent)

    barrier = pltpu.get_barrier_semaphore()
    for axis, me, n in (("sub", sub, ns), ("agg", agg, na)):

        @pl.loop(1, n)
        def _(t, axis=axis, me=me, n=n):
            pl.semaphore_signal(
                barrier, inc=1, device_id={axis: lax.rem(me + t, n)}, device_id_type=MESH
            )

    load_d = pltpu.make_async_copy(dirichlet_hbm, dirichlet_ref, load_sem.at[0])
    load_k = pltpu.make_async_copy(inverse_hbm, inverse_ref, load_sem.at[1])
    load_d.start()
    load_k.start()

    lane = lax.broadcasted_iota(jnp.int32, (1, order), 1)
    mask = jnp.zeros((1, order), F32)
    for k in range(slots):
        inside = (lane >= k * depth) & (lane < k * depth + counts_ref[k])
        mask = mask + jnp.where(inside, 1.0, 0.0)
    mask_ref[...] = jnp.broadcast_to(mask, mask_ref.shape)

    hops = []
    for distance in range(1, reach + 1):
        ahead = lax.rem(sub + distance, ns)
        back = lax.rem(sub + ns - distance, ns)
        hops.append((ahead, back))
        hops.append((back, ahead))
    weights = [
        [jnp.where(peers_ref[k] == to, 1.0, 0.0) for k in range(slots)] for to, _ in hops
    ]

    def face_copy(phase, e):
        return pltpu.make_async_remote_copy(
            src_ref=face_out.at[phase, e],
            dst_ref=face_in.at[phase, e],
            send_sem=face_ss.at[phase, e],
            recv_sem=face_rs.at[phase, e],
            device_id={"sub": hops[e][0]},
            device_id_type=MESH,
        )

    def faces_start(phase):
        for k in range(slots):
            packed_ref[k] = pack(local_ref[:, k * depth : (k + 1) * depth])
        for e in reversed(range(len(hops))):
            total = weights[e][0] * packed_ref[0]
            for k in range(1, slots):
                total = total + weights[e][k] * packed_ref[k]
            face_out[phase, e] = total
            face_copy(phase, e).start()

    def faces_end(phase, out_ref):
        for e in range(len(hops)):
            face_copy(phase, e).wait_recv()
            unsent.append(face_copy(phase, e).wait_send)
        for k in range(0, slots, 2):
            pair = []
            for j in (k, k + 1):
                total = weights[1][j] * face_in[phase, 0]
                for e in range(1, len(hops)):
                    total = total + weights[e ^ 1][j] * face_in[phase, e]
                pair.append(unpack(total, cases, depth))
            at = slice(k * depth, (k + 2) * depth)
            out_ref[:, at] = mask_ref[0:1, at] * (
                local_ref[:, at] + jnp.concatenate(pair, axis=1)
            )

    line = lax.broadcasted_iota(jnp.int32, (cases, 2 * cases), 1)
    case = lax.broadcasted_iota(jnp.int32, (cases, 2 * cases), 0)

    def dots_start(phase, first, second):
        spread = jnp.where(line == case, first, 0.0) + jnp.where(
            line == case + cases, second, 0.0
        )
        total = jnp.sum(spread, axis=0, keepdims=True)
        du_out[phase] = jnp.broadcast_to(total, du_out.shape[1:])
        du_in[phase, sub] = du_out[phase]
        start("sub", lambda p: du_out.at[phase], du_in.at[phase], du_ss.at[phase], du_rs.at[phase])

    def dots_turn(phase):
        receive(
            "sub", lambda p: du_out.at[phase], du_in.at[phase], du_ss.at[phase], du_rs.at[phase]
        )
        dv_out[phase] = jnp.sum(du_in[phase], axis=0)
        dv_in[phase, agg] = dv_out[phase]
        start("agg", lambda p: dv_out.at[phase], dv_in.at[phase], dv_ss.at[phase], dv_rs.at[phase])

    def dots_end(phase):
        receive(
            "agg", lambda p: dv_out.at[phase], dv_in.at[phase], dv_ss.at[phase], dv_rs.at[phase]
        )
        total = jnp.sum(dv_in[phase], axis=0)[0:1]
        first = jnp.sum(jnp.where(line == case, total, 0.0), axis=1, keepdims=True)
        second = jnp.sum(jnp.where(line == case + cases, total, 0.0), axis=1, keepdims=True)
        return first, second

    step = next(w for w in (512, 384, 256, 128, order) if order % w == 0)

    def product(vector, matrix, low, high):
        @pl.loop(low, high)
        def _(c):
            at = pl.ds(pl.multiple_of(c * step, 128), step)
            local_ref[:, at] = dot(vector, matrix[:, at]) * mask_ref[0:1, at]

    chunks = order // step

    local_ref[...] = mask * dual_ref[...]
    pl.semaphore_wait(barrier, ns - 1 + na - 1)
    faces_start(0)

    across = lax.broadcasted_iota(jnp.int32, (primal, primal), 1)
    down = lax.broadcasted_iota(jnp.int32, (primal, primal), 0)
    owner_row = owners_ref[...].astype(F32)
    hot = jnp.where(
        lax.broadcasted_iota(jnp.int32, (8 * pl.cdiv(na, 8), primal), 0)
        == owner_row.astype(jnp.int32),
        1.0,
        0.0,
    )
    before = jnp.where(down < across, 1.0, 0.0).astype(BF16)
    earlier = dot(hot.astype(BF16), before)
    rank = jnp.sum(hot * earlier, axis=0, keepdims=True)
    late = rank >= half
    place_row = (
        owner_row * half + rank + jnp.where(late, float(used - half), 0.0)
    ).astype(jnp.int32)
    place_hot = jnp.where(
        lax.broadcasted_iota(jnp.int32, (2 * used, primal), 0) == place_row, 1.0, 0.0
    )
    place_col = jnp.sum(
        jnp.where(across == down, place_row.astype(F32), 0.0), axis=1, keepdims=True
    ).astype(jnp.int32)
    value_col = jnp.sum(
        jnp.where(across == down, rows_ref[...].astype(F32) + 1.0, 0.0), axis=1, keepdims=True
    )
    spot = lax.broadcasted_iota(jnp.int32, (primal, wide), 1) - agg * half
    fits = (spot >= 0) & (spot < half)
    tile_row = lax.broadcasted_iota(jnp.int32, (8, wide), 0)
    for o in range(na):
        tile = jnp.zeros((8, wide), F32)
        for h in range(2):
            match = fits & (place_col == spot + (h * used + o * half))
            ids = jnp.sum(jnp.where(match, value_col, 0.0), axis=0, keepdims=True)
            tile = tile + jnp.where(tile_row == h, ids, 0.0)
        ida_out[o] = tile
    ida_in[agg] = ida_out[agg]
    start("agg", lambda p: ida_out.at[p], ida_in, ida_ss, ida_rs)
    cp_ref[...] = dot(place_hot.astype(BF16), coupling_ref[...]).astype(BF16)
    b_in[...] = jnp.zeros_like(b_in)
    receive("agg", lambda p: ida_out.at[p], ida_in, ida_ss, ida_rs)
    mine = jnp.sum(ida_in[...], axis=0)
    idb_out[...] = mine
    idb_in[sub] = mine
    start("sub", lambda p: idb_out, idb_in, idb_ss, idb_rs)

    faces_end(0, residual_ref)

    load_d.wait()
    product(residual_ref[...].astype(BF16), dirichlet_ref, 0, chunks)
    rz = 2.0 * jnp.sum(residual_ref[...] * local_ref[...], axis=1, keepdims=True)
    faces_start(1)

    receive("sub", lambda p: idb_out, idb_in, idb_ss, idb_rs)
    coarse = coarse_ref[...]
    coarse_hi = coarse.astype(BF16)
    coarse_lo = (coarse - coarse_hi.astype(F32)).astype(BF16)
    both = jnp.concatenate([coarse_hi, coarse_lo], axis=0)
    index = lax.broadcasted_iota(jnp.int32, (nc, wide), 0).astype(F32) + 1.0

    @pl.loop(0, ns)
    def _(i):
        chosen = jnp.concatenate(
            [
                jnp.where(index == idb_in[i, h : h + 1, :], 1.0, 0.0).astype(BF16)
                for h in range(2)
            ],
            axis=1,
        )
        spread = dot(both, chosen).astype(BF16)
        at = pl.ds(pl.multiple_of(i * wide, 128), wide)
        for h in range(2):
            part = spread[:, h * wide : (h + 1) * wide]
            hi_ref[h * crow : (h + 1) * crow, at] = part[:crow]
            lo_ref[h * crow : (h + 1) * crow, at] = part[crow:]

    fold = crow // 2
    held = ns * fold
    square = lax.broadcasted_iota(jnp.int32, (wide, wide), 0) == lax.broadcasted_iota(
        jnp.int32, (wide, wide), 1
    )
    at_lane = lax.broadcasted_iota(jnp.int32, (used, held), 1)
    number = (at_lane // fold) * crow + at_lane % fold + 1
    for h in range(2):
        ids = idb_out[h : h + 1, :]
        column = jnp.sum(jnp.where(square, ids, 0.0), axis=1, keepdims=True)
        column = column[:used].astype(jnp.int32)
        for g in range(2):
            found = jnp.where(number + g * fold == column, 1.0, 0.0)
            pick_ref[(2 * h + g) * used : (2 * h + g + 1) * used, :] = found.astype(BF16)

    faces_end(1, direction_ref)
    load_k.wait()

    for it in range(ITERS):
        vector = direction_ref[...].astype(BF16)
        terms = lax.dot_general(cp_ref[...], vector, NT, preferred_element_type=F32)
        out = jnp.concatenate([terms[:used], terms[used:]], axis=1)
        a_out[it] = out.reshape(na, half, 2 * cases)
        a_in[it, agg] = a_out[it, agg]
        start("agg", lambda p, it=it: a_out.at[it, p], a_in.at[it], a_ss.at[it], a_rs.at[it])
        product(vector, inverse_ref, 0, chunks // 2)
        receive("agg", lambda p, it=it: a_out.at[it, p], a_in.at[it], a_ss.at[it], a_rs.at[it])
        b_out[it] = a_in[it].reshape(used, 2 * cases)
        b_in[it, sub, 0:used] = b_out[it]

        def b_dst(j, it=it):
            return b_in.at[it, j, pl.ds(0, used)]

        spread_start(b_out.at[it], b_dst, b_ss.at[it], b_rs.at[it])
        product(vector, inverse_ref, chunks // 2, chunks)

        spread_end(b_out.at[it], b_dst, b_ss.at[it], b_rs.at[it])
        given = b_in[it].reshape(ns * wide, 2 * cases)
        given_hi = given.astype(BF16)
        given_lo = (given - given_hi.astype(F32)).astype(BF16)
        solved = (
            dot(hi_ref[...], given_hi) + dot(hi_ref[...], given_lo) + dot(lo_ref[...], given_hi)
        )
        rows = solved[:crow, :cases] + solved[crow:, cases:]
        s_out[it] = jnp.concatenate([rows[:fold], rows[fold:]], axis=1)
        s_in[it, sub] = s_out[it]

        def s_dst(j, it=it):
            return s_in.at[it, j]

        spread_start(s_out.at[it], s_dst, s_ss.at[it], s_rs.at[it])
        spread_end(s_out.at[it], s_dst, s_ss.at[it], s_rs.at[it])
        found = dot(pick_ref[...], s_in[it].reshape(held, 2 * cases).astype(BF16))
        answer = jnp.concatenate(
            [
                found[2 * h * used : (2 * h + 1) * used, :cases]
                + found[(2 * h + 1) * used : (2 * h + 2) * used, cases:]
                for h in range(2)
            ],
            axis=1,
        )
        r_out[it] = answer.reshape(na, half, 2 * cases)
        r_in[it, agg] = r_out[it, agg]
        start("agg", lambda p, it=it: r_out.at[it, p], r_in.at[it], r_ss.at[it], r_rs.at[it])
        receive("agg", lambda p, it=it: r_out.at[it, p], r_in.at[it], r_ss.at[it], r_rs.at[it])
        came = r_in[it].reshape(used, 2 * cases)
        back = jnp.concatenate([came[:, :cases], came[:, cases:]], axis=0)
        back = jnp.transpose(back).astype(BF16)

        @pl.loop(0, chunks)
        def _(c):
            at = pl.ds(pl.multiple_of(c * step, 128), step)
            local_ref[:, at] += dot(back, cp_ref[:, at]) * mask_ref[0:1, at]

        image_dot = 2.0 * jnp.sum(direction_ref[...] * local_ref[...], axis=1, keepdims=True)
        phase = 2 * it
        dots_start(phase, rz, image_dot)
        faces_start(2 + phase)
        dots_turn(phase)
        faces_end(2 + phase, field_ref)
        first, second = dots_end(phase)
        if it == 0:
            rz = first
        else:
            rz = rz_all
        alpha = rz / second
        if it == 0:
            solution_ref[...] = alpha * direction_ref[...]
        else:
            solution_ref[...] += alpha * direction_ref[...]
        residual_ref[...] -= alpha * field_ref[...]
        if it + 1 < ITERS:
            product(residual_ref[...].astype(BF16), dirichlet_ref, 0, chunks)
            part = 2.0 * jnp.sum(residual_ref[...] * local_ref[...], axis=1, keepdims=True)
            dots_start(phase + 1, part, part)
            faces_start(3 + phase)
            dots_turn(phase + 1)
            faces_end(3 + phase, field_ref)
            rz_all = dots_end(phase + 1)[0]
            direction_ref[...] = field_ref[...] + (rz_all / rz) * direction_ref[...]

    for sent in unsent:
        sent()


def shards(
    dual_load,
    interface_inverse,
    dirichlet,
    coupling,
    neighbours,
    face_counts,
    owners,
    primal_rows,
    coarse_inverse,
):
    ns = lax.axis_size("sub")
    na = lax.axis_size("agg")
    reach = min(4, (ns - 1) // 2)
    cases, order = dual_load.shape[2:]
    slots = neighbours.shape[2]
    depth = order // slots
    crow, nc = coarse_inverse.shape[1:]
    half = CAP // 2
    used = na * half
    wide = pl.cdiv(used, 128) * 128
    lanes = 2 * cases
    face_rows = cases * depth // 128
    phases = 2 * ITERS + 1
    dots = 2 * ITERS - 1
    dma = pltpu.SemaphoreType.DMA

    def exchange(times, n, out, rows):
        return [
            pltpu.VMEM(out, F32),
            pltpu.VMEM(rows, F32),
            dma((times, n - 1) if times else (n - 1,)),
            dma((times, n - 1) if times else (n - 1,)),
        ]

    scratch = [
        pltpu.VMEM((order, order), BF16),
        pltpu.VMEM((order, order), BF16),
        pltpu.VMEM((cases, order), F32),
        pltpu.VMEM((cases, order), F32),
        pltpu.VMEM((cases, order), F32),
        pltpu.VMEM((slots, face_rows, 128), F32),
        pltpu.VMEM((phases, 2 * reach, face_rows, 128), F32),
        pltpu.VMEM((phases, 2 * reach, face_rows, 128), F32),
        dma((phases, 2 * reach)),
        dma((phases, 2 * reach)),
        dma((2,)),
        pltpu.VMEM((2 * used, order), BF16),
        pltpu.VMEM((8, order), F32),
        *exchange(0, na, (na, 8, wide), (na, 8, wide)),
        *exchange(0, ns, (8, wide), (ns, 8, wide)),
        pltpu.VMEM((2 * crow, ns * wide), BF16),
        pltpu.VMEM((2 * crow, ns * wide), BF16),
        pltpu.VMEM((4 * used, ns * crow // 2), BF16),
        *exchange(ITERS, na, (ITERS, na, half, lanes), (ITERS, na, half, lanes)),
        *exchange(ITERS, ns, (ITERS, used, lanes), (ITERS, ns, wide, lanes)),
        *exchange(ITERS, ns, (ITERS, crow // 2, lanes), (ITERS, ns, crow // 2, lanes)),
        *exchange(ITERS, na, (ITERS, na, half, lanes), (ITERS, na, half, lanes)),
        *exchange(dots, ns, (dots, 8, lanes), (dots, ns, 8, lanes)),
        *exchange(dots, na, (dots, 8, lanes), (dots, na, 8, lanes)),
    ]
    vmem = pl.BlockSpec(memory_space=pltpu.VMEM)
    smem = pl.BlockSpec(memory_space=pltpu.SMEM)
    anywhere = pl.BlockSpec(memory_space=pl.ANY)
    shape = jax.ShapeDtypeStruct((cases, order), F32)
    solved, left = pl.pallas_call(
        functools.partial(kernel, ns, na, reach),
        out_shape=(shape, shape),
        in_specs=[vmem, anywhere, anywhere, vmem, smem, smem, vmem, vmem, vmem],
        out_specs=(vmem, vmem),
        scratch_shapes=scratch,
        compiler_params=pltpu.CompilerParams(
            collective_id=0, has_side_effects=True, vmem_limit_bytes=56 * 1024 * 1024
        ),
    )(
        dual_load[0, 0],
        interface_inverse[0, 0],
        dirichlet[0, 0],
        coupling[0, 0],
        neighbours[0, 0],
        face_counts[0, 0],
        owners[0, 0].reshape(1, -1),
        primal_rows[0],
        coarse_inverse[0],
    )
    return solved[None, None], left[None, None]


def solution(mesh):
    in_specs = (
        P("agg", "sub", None, None),
        P("agg", "sub", None, None),
        P("agg", "sub", None, None),
        P("agg", "sub", None, None),
        P("agg", "sub", None),
        P("agg", "sub", None),
        P("agg", "sub", None, None),
        P("agg", "sub", None),
        P("agg", "sub", None),
    )
    out_specs = (P("agg", "sub", None, None), P("agg", "sub", None, None))
    return jax.shard_map(shards, mesh=mesh, in_specs=in_specs, out_specs=out_specs, check_vma=False)
```
